512 devices in a mesh: ia: 16 (over z), ja: 8 (over y, core), ka: 4 (over x).
Axes of the slice: x: 4, y: 4, z: 16, core: 2. Of those that a mesh axis runs over, the one named last changes fastest.
Arguments:
- tensor_tiles: bfloat16 [16, 8, 4, 8, 64, 4096], P('ia', 'ja', 'ka'), may hold values from -6 to 6
- item_rows: bfloat16 [1024, 64, 128], P(('ia', 'ja')), may hold values from -0.75 to 0.75
- word_rows: bfloat16 [128, 64, 128], P(('ia', 'ka')), may hold values from -0.75 to 0.75
- heavy_local: int32 [16, 8, 1], P('ia', 'ja'), may hold values from 0 to 7
- send_blocks: int32 [16, 8, 4, 16, 1], P('ia', 'ja', 'ka'), may hold values from 0 to 7
- tile_slot: int32 [16, 8, 4, 8], P('ia', 'ja', 'ka'), may hold values from 0 to 31
- tile_word: int32 [16, 8, 4, 8], P('ia', 'ja', 'ka'), may hold values from 0 to 31
- tile_user: int32 [16, 8, 4, 8], P('ia', 'ja', 'ka'), may hold values from 0 to 31, as said below
- tile_count: int32 [16, 8, 4], P('ia', 'ja', 'ka'), may hold values from 1 to 8
Outputs:
- user_panel: float32 [512, 64, 128], P(('ia', 'ja', 'ka'))
The draws below stay inside these ranges and needn't reach their ends.
Inputs may be any that keep to these rules, and one draw needn't show every extreme that they name: The tiles of one device name different user blocks: tile_user differs between any two tiles of one device.
All inputs are finite; a program needn't handle non-finite values.
Results may differ from the reference program's by a relative error of at most 0.0029.
Values may be sent and summed in bfloat16 or wider, within the bound.
A program may use at most 64 MiB of HBM per device.

```python
import jax
import jax.numpy as jnp
from jax import lax

E = 64
R = 128
TILES_DEV = 8
VB_DEV = 8
WB_DEV = 2
UB_DEV = 1
HV_DEV = 1
SLOTS = 1
UB_I = 32
UB = 512
VB = 1024
WB = 128
TABLE = 32
N_IA = 16
N_JA = 8
N_KA = 4


def draw_tile_user(key, part):
    owners_all = N_JA * N_KA
    key_order = jax.random.fold_in(key, 11)
    key_local = jax.random.fold_in(key, 12)
    scores = jax.random.randint(key_order, (N_IA, N_JA, N_KA, owners_all), 0, 1 << 20) * owners_all + jnp.arange(owners_all, dtype=jnp.int32)
    order = jnp.argsort(scores, axis=-1, stable=True).astype(jnp.int32)
    owners = order[..., :TILES_DEV]
    local_ids = jax.random.randint(key_local, (N_IA, N_JA, N_KA, TILES_DEV), 0, UB_DEV)
    return (owners * UB_DEV + local_ids).astype(jnp.int32)


def touch_ends(result, stream_key, smallest, largest):
    longest = result.shape.index(max(result.shape))
    spots = []
    for shift in (0, 1):
        where = [jax.random.randint(jax.random.fold_in(stream_key, axis), (), 0, length) for axis, length in enumerate(result.shape)]
        where[longest] = (where[longest] + shift) % result.shape[longest]
        spots.append(tuple(where))
    return result.at[spots[0]].set(smallest).at[spots[1]].set(largest)


def block_levels(key, extent, shards, smallest, top_value):
    gain, own = 1.0, jax.random.fold_in(key, 6)
    for position, parts in shards:
        heights = jnp.exp(jax.random.uniform(jax.random.fold_in(own, position), (parts,), jnp.float32, smallest / len(shards), top_value / len(shards)))
        gain = gain * jnp.repeat(heights, extent[position] // parts).reshape([-1 if axis == position else 1 for axis in range(len(extent))])
    return gain


def scatter_about(own_key, shape, scale, limit, shards=(), kind=jnp.bfloat16):
    array = scale * jax.random.normal(own_key, shape, jnp.float32)
    if shards:
        array = array * block_levels(own_key, shape, shards, -0.22, 0.18)
    return jnp.clip(array, -limit, limit).astype(kind)


def setup_inputs(seed: int = 0) -> dict:
    splits = jax.random.split(jax.random.key(seed), 10)
    return {
        "tensor_tiles": scatter_about(splits[0], (N_IA, N_JA, N_KA, TILES_DEV, E, E * E), 1.0, 6.0, ((0, 16), (1, 8), (2, 4))),
        "item_rows": scatter_about(splits[1], (VB, E, R), E ** -0.5, 0.75, ((0, 128),)),
        "word_rows": scatter_about(splits[2], (WB, E, R), E ** -0.5, 0.75, ((0, 64),)),
        "heavy_local": touch_ends(jax.random.randint(splits[3], (N_IA, N_JA, HV_DEV), 0, VB_DEV), jax.random.fold_in(splits[3], 1), 0, VB_DEV - 1).astype(jnp.int32),
        "send_blocks": touch_ends(jax.random.randint(splits[4], (N_IA, N_JA, N_KA, N_IA, SLOTS), 0, VB_DEV), jax.random.fold_in(splits[4], 1), 0, VB_DEV - 1).astype(jnp.int32),
        "tile_slot": touch_ends(jax.random.randint(splits[5], (N_IA, N_JA, N_KA, TILES_DEV), 0, TABLE), jax.random.fold_in(splits[5], 1), 0, TABLE - 1).astype(jnp.int32),
        "tile_word": touch_ends(jax.random.randint(splits[6], (N_IA, N_JA, N_KA, TILES_DEV), 0, N_IA * WB_DEV), jax.random.fold_in(splits[6], 1), 0, (N_IA * WB_DEV) - 1).astype(jnp.int32),
        "tile_user": draw_tile_user(jax.random.fold_in(splits[9], 71), 0),
        "tile_count": touch_ends(jax.random.randint(splits[8], (N_IA, N_JA, N_KA), 1, TILES_DEV + 1), jax.random.fold_in(splits[8], 1), 1, TILES_DEV).astype(jnp.int32),
    }


def device_partial(row_group, col_group, dep_group, tensor_tiles, item_view, word_view, heavy_local, send_blocks, tile_slot, tile_word, tile_user, tile_count):
    peers = jnp.arange(N_IA)[:, None]
    heavy = item_view[peers, col_group, heavy_local[:, col_group, :]]
    light = item_view[peers, col_group, send_blocks[:, col_group, dep_group, row_group, :]]
    table = jnp.concatenate([heavy.reshape(-1, E, R), light.reshape(-1, E, R)], axis=0)
    item_tile = table[tile_slot[row_group, col_group, dep_group]]
    words = word_view[:, dep_group].reshape(N_IA * WB_DEV, E, R)
    word_tile = words[tile_word[row_group, col_group, dep_group]]
    krao = (item_tile.astype(jnp.float32)[:, :, None, :] * word_tile.astype(jnp.float32)[:, None, :, :]).astype(jnp.bfloat16)
    krao = krao.reshape(TILES_DEV, E * E, R)
    block = tensor_tiles[row_group, col_group, dep_group]
    contrib = jnp.einsum("tab,tbr->tar", block.astype(jnp.float32), krao.astype(jnp.float32))
    live = (jnp.arange(TILES_DEV) < tile_count[row_group, col_group, dep_group]).astype(jnp.float32)
    contrib = contrib * live[:, None, None]
    onehot = (tile_user[row_group, col_group, dep_group][None, :] == jnp.arange(UB_I)[:, None]).astype(jnp.float32)
    return jnp.einsum("ut,tar->uar", onehot, contrib, precision=lax.Precision.HIGHEST)


def reference(tensor_tiles, item_rows, word_rows, heavy_local, send_blocks, tile_slot, tile_word, tile_user, tile_count):
    item_view = item_rows.reshape(N_IA, N_JA, VB_DEV, E, R)
    word_view = word_rows.reshape(N_IA, N_KA, WB_DEV, E, R)

    def one_group(row_group):
        def accumulate(total, pair):
            col_group = pair // N_KA
            dep_group = pair % N_KA
            part = device_partial(row_group, col_group, dep_group, tensor_tiles, item_view, word_view, heavy_local, send_blocks, tile_slot, tile_word, tile_user, tile_count)
            return total + part, None

        total, _ = lax.scan(accumulate, jnp.zeros((UB_I, E, R), jnp.float32), jnp.arange(N_JA * N_KA))
        return total

    groups = lax.map(one_group, jnp.arange(N_IA))
    return groups.reshape(UB, E, R)
```

```python
import functools

import jax
import jax.numpy as jnp
from jax import lax
from jax.experimental import pallas as pl
from jax.experimental.pallas import tpu as pltpu
from jax.sharding import PartitionSpec as P

MESH = pl.DeviceIdType.MESH
NZ, NX, NY, NC = 16, 4, 4, 2
TILES = 8
E = 64
R = 128
Q = E // NX
BF = jnp.bfloat16
F32 = jnp.float32
Z_ORDER = (8, 7, 9, 6, 10, 5, 11, 4, 12, 3, 13, 2, 14, 1, 15)


def remote(src, dst, send_sem, recv_sem, device):
    return pltpu.make_async_remote_copy(
        src_ref=src, dst_ref=dst, send_sem=send_sem, recv_sem=recv_sem, device_id=device, device_id_type=MESH
    )


def kernel(
    tiles_hbm, item_hbm, word_hbm, heavy_hbm, send_hbm, slot_hbm, tword_hbm, user_hbm, count_hbm,
    out_ref,
    tiles, items, gath, table, words, light, item32, krao, contrib, pair_out, pair_in, plane_out, plane_in, own,
    heavy_s, send_s, slot_s, tword_s, user_s, count_s, inv_s,
    tile_sem, load_sem, int_sem,
    zg_send, zg_recv, zl_send, zl_recv, x_send, x_recv, y_send, y_recv, c_send, c_recv, p_send, p_recv, q_send, q_recv,
):
    i = lax.axis_index("ia")
    j = lax.axis_index("ja")
    k = lax.axis_index("ka")
    y = j // 2
    c = lax.rem(j, 2)
    chip = y * NX + k

    def zpeer(d):
        return lax.rem(i + d, NZ)

    def chip_dev(q):
        return {"ja": (q // NX) * 2 + c, "ka": lax.rem(q, NX)}

    other = {"ja": y * 2 + 1 - c}

    ints = [
        pltpu.make_async_copy(a, b, int_sem.at[n])
        for n, (a, b) in enumerate(
            (
                (heavy_hbm, heavy_s), (send_hbm, send_s), (slot_hbm, slot_s),
                (tword_hbm, tword_s), (user_hbm, user_s), (count_hbm, count_s),
            )
        )
    ]
    for cp in ints:
        cp.start()
    load_items = pltpu.make_async_copy(item_hbm, items, load_sem.at[0])
    load_items.start()
    kq = pl.multiple_of(k * Q, Q)
    yq = pl.multiple_of(y * Q, Q)
    load_word = pltpu.make_async_copy(word_hbm.at[c, pl.ds(yq, Q)], gath.at[i, 1], load_sem.at[1])
    load_word.start()

    barrier = pltpu.get_barrier_semaphore()
    for d in Z_ORDER:
        pl.semaphore_signal(barrier, inc=1, device_id={"ia": zpeer(d)}, device_id_type=MESH)
    for d in range(1, 16):
        pl.semaphore_signal(barrier, inc=1, device_id=chip_dev(lax.rem(chip + d, 16)), device_id_type=MESH)
    pl.semaphore_signal(barrier, inc=1, device_id=other, device_id_type=MESH)

    tile_loads = [pltpu.make_async_copy(tiles_hbm.at[0, 0, 0, t], tiles.at[t], tile_sem.at[t]) for t in range(TILES)]
    for cp in tile_loads:
        cp.start()

    for cp in ints:
        cp.wait()
    load_items.wait()
    load_word.wait()
    gath[i, 0] = items[heavy_s[0, 0, 0], pl.ds(kq, Q), :]
    for p in range(NZ):
        light[p] = items[send_s[0, 0, 0, p]]
    table[NZ + i] = items[send_s[0, 0, 0, i]]

    count = count_s[0, 0, 0]

    def find(u, carry):
        at = jnp.int32(TILES)
        for t in range(TILES):
            at = jnp.where((user_s[0, 0, 0, t] == u) & (count > t), t, at)
        inv_s[u] = at
        return carry

    lax.fori_loop(0, NX * NY * NC, find, 0)
    contrib[TILES] = jnp.zeros((E, R), F32)

    pl.semaphore_wait(barrier, 31)

    zg = [
        remote(gath.at[i], gath.at[i], zg_send.at[d], zg_recv.at[d], {"ia": zpeer(d)}) for d in Z_ORDER
    ]
    for cp in zg:
        cp.start()
    zl = [
        remote(light.at[zpeer(d)], table.at[NZ + i], zl_send.at[d], zl_recv.at[d], {"ia": zpeer(d)}) for d in Z_ORDER
    ]
    for cp in zl:
        cp.start()

    for cp in zg:
        cp.wait_recv()
    xs = [
        remote(gath.at[:, 0], table.at[pl.ds(0, NZ), pl.ds(kq, Q)], x_send.at[d], x_recv.at[d], {"ka": lax.rem(k + d, NX)})
        for d in (2, 1, 3)
    ]
    ys = [
        remote(gath.at[:, 1], words.at[:, c, pl.ds(yq, Q)], y_send.at[d], y_recv.at[d], {"ja": lax.rem(j + 2 * d, 8)})
        for d in (2, 1, 3)
    ]
    for a, b in zip(xs, ys):
        a.start()
        b.start()
    for p in range(NZ):
        table[p, pl.ds(kq, Q), :] = gath[p, 0]
        words[p, c, pl.ds(yq, Q), :] = gath[p, 1]
    for cp in ys:
        cp.wait_recv()
    cx = remote(words.at[:, c], words.at[:, c], c_send.at[0], c_recv.at[0], other)
    cx.start()
    for cp in xs:
        cp.wait_recv()
    for cp in zl:
        cp.wait_recv()
    cx.wait_recv()
    for cp in tile_loads:
        cp.wait()

    def one_tile(t, carry):
        item32[...] = table[slot_s[0, 0, 0, t]].astype(F32)
        q = tword_s[0, 0, 0, t]
        word = words[q >> 1, q & 1]
        for b in range(E):
            row = jnp.broadcast_to(item32[pl.ds(b, 1), :], (E, R)).astype(BF)
            krao[pl.ds(b * E, E), :] = row * word
        contrib[t] = jnp.dot(tiles[t], krao[...], preferred_element_type=F32)
        return carry

    lax.fori_loop(0, TILES, one_tile, 0)

    def to_pair(q, carry):
        pair_out[q] = contrib[inv_s[(q // NX) * 8 + (1 - c) * NX + lax.rem(q, NX)]].astype(BF)
        return carry

    lax.fori_loop(0, 16, to_pair, 0)
    px = remote(pair_out, pair_in, p_send.at[0], p_recv.at[0], other)
    px.start()
    px.wait_recv()

    for d in range(1, 16):
        q = lax.rem(chip + d, 16)
        mine = contrib[inv_s[(q // NX) * 8 + c * NX + lax.rem(q, NX)]]
        plane_out[q] = (mine + pair_in[q].astype(F32)).astype(BF)
        remote(plane_out.at[q], plane_in.at[d], q_send.at[d], q_recv.at[d], chip_dev(q)).start()
    own[...] = contrib[inv_s[y * 8 + c * NX + k]] + pair_in[chip].astype(F32)

    for d in range(1, 16):
        q = lax.rem(chip + d, 16)
        remote(plane_out.at[q], plane_in.at[d], q_send.at[d], q_recv.at[d], chip_dev(q)).wait_recv()
        own[...] += plane_in[d].astype(F32)
    out_ref[0] = own[...]

    for cp in zg + zl + xs + ys + [cx, px]:
        cp.wait_send()
    for d in range(1, 16):
        q = lax.rem(chip + d, 16)
        remote(plane_out.at[q], plane_in.at[d], q_send.at[d], q_recv.at[d], chip_dev(q)).wait_send()


def local(*args):
    args = list(args)
    args[4] = args[4].reshape(1, 1, 1, NZ)
    dma = pltpu.SemaphoreType.DMA
    return pl.pallas_call(
        kernel,
        out_shape=jax.ShapeDtypeStruct((1, E, R), F32),
        in_specs=[pl.BlockSpec(memory_space=pltpu.HBM)] * 9,
        out_specs=pl.BlockSpec(memory_space=pltpu.VMEM),
        scratch_shapes=[
            pltpu.VMEM((TILES, E, E * E), BF),
            pltpu.VMEM((8, E, R), BF),
            pltpu.VMEM((NZ, 2, Q, R), BF),
            pltpu.VMEM((2 * NZ, E, R), BF),
            pltpu.VMEM((NZ, 2, E, R), BF),
            pltpu.VMEM((NZ, E, R), BF),
            pltpu.VMEM((E, R), F32),
            pltpu.VMEM((E * E, R), BF),
            pltpu.VMEM((TILES + 1, E, R), F32),
            pltpu.VMEM((16, E, R), BF),
            pltpu.VMEM((16, E, R), BF),
            pltpu.VMEM((16, E, R), BF),
            pltpu.VMEM((16, E, R), BF),
            pltpu.VMEM((E, R), F32),
            pltpu.SMEM((1, 1, 1), jnp.int32),
            pltpu.SMEM((1, 1, 1, NZ), jnp.int32),
            pltpu.SMEM((1, 1, 1, TILES), jnp.int32),
            pltpu.SMEM((1, 1, 1, TILES), jnp.int32),
            pltpu.SMEM((1, 1, 1, TILES), jnp.int32),
            pltpu.SMEM((1, 1, 1), jnp.int32),
            pltpu.SMEM((32,), jnp.int32),
            dma((TILES,)), dma((2,)), dma((6,)),
            dma((16,)), dma((16,)), dma((16,)), dma((16,)),
            dma((4,)), dma((4,)), dma((4,)), dma((4,)),
            dma((1,)), dma((1,)), dma((1,)), dma((1,)),
            dma((16,)), dma((16,)),
        ],
        compiler_params=pltpu.CompilerParams(collective_id=0, has_side_effects=True, vmem_limit_bytes=32 << 20),
        name="mttkrp",
    )(*args)


def solution(mesh):
    return jax.shard_map(
        local,
        mesh=mesh,
        in_specs=(
            P("ia", "ja", "ka", None, None, None),
            P(("ia", "ja"), None, None),
            P(("ia", "ka"), None, None),
            P("ia", "ja", None),
            P("ia", "ja", "ka", None, None),
            P("ia", "ja", "ka", None),
            P("ia", "ja", "ka", None),
            P("ia", "ja", "ka", None),
            P("ia", "ja", "ka"),
        ),
        out_specs=P(("ia", "ja", "ka"), None, None),
        check_vma=False,
    )
```

```python
import jax
import jax.numpy as jnp
from jax import lax
from jax.experimental import pallas as pl
from jax.experimental.pallas import tpu as pltpu
from jax.sharding import PartitionSpec as P

MESH = pl.DeviceIdType.MESH
NZ, NX, NY, NC = 16, 4, 4, 2
TILES = 8
E = 64
R = 128
Q = E // NX
H = E // 2
BF = jnp.bfloat16
F32 = jnp.float32
NEAR = (0, 1, 15, 2, 14, 4, 12)
FAR = (3, 13, 5, 11, 6, 10, 7, 9, 8)
POS = {r: n for n, r in enumerate(NEAR + FAR)}
SPLIT = len(NEAR)
HEAVY, COUNT = 0, 1


def kernel(
    tiles_hbm, item_hbm, word_hbm, pair_hbm, send_hbm, slot_hbm, tword_hbm, user_hbm,
    out_ref,
    tiles, items, gath, table, words, light, relay, item32, krao_a, krao_b, contrib, pcontrib, plane_out, plane_in,
    pair_s, send_s, slot_s, tword_s, user_s, ppair_s, puser_s, pos_s, inv_s, pinv_s,
    tile_sem, load_sem, ss, rs, t_send, t_recv, q_send, q_recv,
):
    i = lax.axis_index("ia")
    j = lax.axis_index("ja")
    k = lax.axis_index("ka")
    y = j // 2
    c = lax.rem(j, 2)
    chip = y * NX + k
    kq = pl.multiple_of(k * Q, Q)
    yq = pl.multiple_of(y * Q, Q)

    def zdev(d):
        return {"ia": lax.rem(i + (d % NZ), NZ)}

    def chip_dev(q):
        return {"ja": (q // NX) * 2 + c, "ka": lax.rem(q, NX)}

    other = {"ja": y * 2 + 1 - c}
    used = [0]

    def remote(src, dst, device):
        n = used[0]
        used[0] += 1
        return pltpu.make_async_remote_copy(
            src_ref=src, dst_ref=dst, send_sem=ss.at[n], recv_sem=rs.at[n], device_id=device, device_id_type=MESH
        )

    load_items = pltpu.make_async_copy(item_hbm, items, load_sem.at[0])
    load_word = pltpu.make_async_copy(word_hbm.at[c, pl.ds(yq, Q)], gath.at[0, 1], load_sem.at[1])
    ints = ((pair_hbm, pair_s), (send_hbm, send_s), (slot_hbm, slot_s), (tword_hbm, tword_s), (user_hbm, user_s))
    ints = [pltpu.make_async_copy(a, b, load_sem.at[2 + n]) for n, (a, b) in enumerate(ints)]
    for cp in ints:
        cp.start()
    load_items.start()
    load_word.start()

    barrier = pltpu.get_barrier_semaphore()
    for d in (4, -4, 3, -3, 2, -2, 1, -1):
        pl.semaphore_signal(barrier, inc=1, device_id=zdev(d), device_id_type=MESH)
    for d in range(1, 16):
        pl.semaphore_signal(barrier, inc=1, device_id=chip_dev(lax.rem(chip + d, 16)), device_id_type=MESH)
    pl.semaphore_signal(barrier, inc=1, device_id=other, device_id_type=MESH)

    tile_loads = [pltpu.make_async_copy(tiles_hbm.at[0, 0, 0, t], tiles.at[t], tile_sem.at[t]) for t in range(TILES)]
    for cp in tile_loads:
        cp.start()
    for r, n in POS.items():
        pos_s[r] = n

    for cp in ints:
        cp.wait()
    load_items.wait()
    load_word.wait()
    gath[0, 0] = items[pair_s[0, HEAVY], pl.ds(kq, Q), :]
    for d in range(1, NZ):
        light[d] = items[send_s[0, 0, 0, lax.rem(i + d, NZ)]]
    table[NZ] = items[send_s[0, 0, 0, i]]

    def find(pair, user, inv):
        count = pair[0, COUNT]

        def body(n, carry):
            u = (n // NX) * (NC * NX) + c * NX + lax.rem(n, NX)
            at = jnp.int32(TILES)
            for t in range(TILES):
                at = jnp.where((user[0, 0, 0, t] == u) & (count > t), t, at)
            inv[n] = at
            return carry

        lax.fori_loop(0, NX * NY, body, 0)

    find(pair_s, user_s, inv_s)
    contrib[TILES] = jnp.zeros((E, R), F32)
    pcontrib[TILES] = jnp.zeros((E, R), F32)

    pl.semaphore_wait(barrier, 24)

    def direct(d):
        return remote(gath.at[0], gath.at[POS[-d % NZ]], zdev(d))

    ag = {-d % NZ: direct(d) for d in (4, -4, 2, -2, 1, -1)}
    for cp in ag.values():
        cp.start()

    up = [remote(light.at[8, pl.ds(0, H)], relay.at[0, 3, pl.ds(0, H)], zdev(4))]
    down = [remote(light.at[8, pl.ds(H, H)], relay.at[1, 3, pl.ds(H, H)], zdev(-4))]
    for f in (3, 2, 1):
        up.append(remote(light.at[4 + f], relay.at[0, f - 1], zdev(4)))
        down.append(remote(light.at[NZ - 4 - f], relay.at[1, f - 1], zdev(-4)))
    for a, b in zip(up, down):
        a.start()
        b.start()
    px = [remote(pair_hbm, ppair_s, other), remote(user_hbm, puser_s, other)]
    for cp in px:
        cp.start()

    ag[12].wait_recv()
    ag[4].wait_recv()
    hops = [
        remote(gath.at[POS[12], 0], gath.at[POS[8], 0], zdev(4)),
        remote(gath.at[POS[4], 1], gath.at[POS[8], 1], zdev(-4)),
    ]
    for f in (3, 2, 1):
        hops.append(remote(gath.at[POS[12]], gath.at[POS[12 - f]], zdev(f)))
        hops.append(remote(gath.at[POS[4]], gath.at[POS[4 + f]], zdev(-f)))
    hops.append(remote(gath.at[POS[12]], gath.at[POS[13]], zdev(-1)))
    hops.append(remote(gath.at[POS[4]], gath.at[POS[3]], zdev(1)))
    for cp in hops:
        cp.start()

    near = [remote(light.at[d % NZ], table.at[NZ + (-d % NZ)], zdev(d)) for d in (4, -4, 3, -3, 2, -2, 1, -1)]
    for cp in near:
        cp.start()

    def spread(lo, n):
        out = []
        for d in (2, 1, 3):
            out.append(
                remote(
                    gath.at[pl.ds(lo, n), 1], words.at[pl.ds(lo, n), c, pl.ds(yq, Q)], {"ja": lax.rem(j + 2 * d, NY * NC)}
                )
            )
            out.append(
                remote(gath.at[pl.ds(lo, n), 0], table.at[pl.ds(lo, n), pl.ds(kq, Q)], {"ka": lax.rem(k + d, NX)})
            )
        for cp in out:
            cp.start()
        for n in range(lo, lo + n):
            table[n, pl.ds(kq, Q), :] = gath[n, 0]
            words[n, c, pl.ds(yq, Q), :] = gath[n, 1]
        return out

    for r in (14, 2, 15, 1):
        ag[r].wait_recv()
    spread_a = spread(0, SPLIT)

    fwd = []
    for n, f in enumerate((4, 3, 2, 1)):
        rows = (pl.ds(0, H), pl.ds(H, H)) if f == 4 else (pl.ds(0, E), pl.ds(0, E))
        up[n].wait_recv()
        fwd.append(remote(relay.at[0, f - 1, rows[0]], table.at[NZ + 12 - f, rows[0]], zdev(f)))
        fwd[-1].start()
        down[n].wait_recv()
        fwd.append(remote(relay.at[1, f - 1, rows[1]], table.at[NZ + 4 + f, rows[1]], zdev(-f)))
        fwd[-1].start()

    for cp in hops:
        cp.wait_recv()
    spread_b = spread(SPLIT, NZ - SPLIT)

    def pair_words(sent, lo, n):
        for cp in sent[0::2]:
            cp.wait_recv()
        cp = remote(words.at[pl.ds(lo, n), c], words.at[pl.ds(lo, n), c], other)
        cp.start()
        return cp

    pw = [pair_words(spread_a, 0, SPLIT), pair_words(spread_b, SPLIT, NZ - SPLIT)]
    for cp in px:
        cp.wait_recv()
    find(ppair_s, puser_s, pinv_s)
    for cp in spread_a[1::2] + spread_b[1::2] + near + fwd + pw:
        cp.wait_recv()
    for cp in tile_loads:
        cp.wait()

    def build(t, krao):
        s = slot_s[0, 0, 0, t]
        r = (s - i) & (NZ - 1)
        item32[...] = table[jnp.where(s < NZ, pos_s[r], NZ + r)].astype(F32)
        q = tword_s[0, 0, 0, t]
        word = words[pos_s[((q >> 1) - i) & (NZ - 1)], q & 1]
        for b in range(E):
            row = jnp.broadcast_to(item32[pl.ds(b, 1), :], (E, R)).astype(BF)
            krao[pl.ds(b * E, E), :] = row * word

    groups = ((0, 4), (4, 8))

    def send_tiles(n):
        lo, hi = groups[n]
        return pltpu.make_async_remote_copy(
            src_ref=contrib.at[pl.ds(lo, hi - lo)], dst_ref=pcontrib.at[pl.ds(lo, hi - lo)],
            send_sem=t_send.at[n], recv_sem=t_recv.at[n], device_id=other, device_id_type=MESH,
        )

    build(0, krao_a)
    for n, (lo, hi) in enumerate(groups):
        for t in range(lo, hi):
            now, later = (krao_a, krao_b) if t % 2 == 0 else (krao_b, krao_a)
            contrib[t] = jnp.dot(tiles[t], now[...], preferred_element_type=F32)
            if t + 1 < TILES:
                build(t + 1, later)
        send_tiles(n).start()
    for n in range(len(groups)):
        send_tiles(n).wait_recv()

    def plane(d):
        q = lax.rem(chip + d, 16)
        return q, pltpu.make_async_remote_copy(
            src_ref=plane_out.at[d], dst_ref=plane_in.at[d], send_sem=q_send.at[d], recv_sem=q_recv.at[d],
            device_id=chip_dev(q), device_id_type=MESH,
        )

    far_first = (10, 6, 14, 9, 11, 2, 8, 5, 7, 13, 15, 1, 3, 4, 12)
    for d in far_first:
        q, cp = plane(d)
        plane_out[d] = (contrib[inv_s[q]] + pcontrib[pinv_s[q]]).astype(BF)
        cp.start()
    total = contrib[inv_s[chip]] + pcontrib[pinv_s[chip]]
    for d in far_first[::-1]:
        plane(d)[1].wait_recv()
        total = total + plane_in[d].astype(F32)
    out_ref[0] = total

    for cp in list(ag.values()) + up + down + px + hops + near + spread_a + spread_b + fwd + pw:
        cp.wait_send()
    for n in range(len(groups)):
        send_tiles(n).wait_send()
    for d in far_first:
        plane(d)[1].wait_send()


def local(tiles, items, word_rows, heavy, send, slot, tword, user, count):
    dma = pltpu.SemaphoreType.DMA
    lane = lax.broadcasted_iota(jnp.int32, (1, R), 1)
    pair = jnp.where(lane == HEAVY, heavy.reshape(1, 1), count.reshape(1, 1))
    ints = (pair, send.reshape(1, 1, 1, NZ), slot, tword, user)
    args = [pltpu.with_memory_space_constraint(a, pltpu.HBM) for a in (tiles, items, word_rows, *ints)]
    return pl.pallas_call(
        kernel,
        out_shape=pltpu.VMEM((1, E, R), F32),
        in_specs=[pl.BlockSpec(memory_space=pltpu.HBM)] * 8,
        out_specs=pl.BlockSpec(memory_space=pltpu.VMEM),
        scratch_shapes=[
            pltpu.VMEM((TILES, E, E * E), BF),
            pltpu.VMEM((8, E, R), BF),
            pltpu.VMEM((NZ, 2, Q, R), BF),
            pltpu.VMEM((2 * NZ, E, R), BF),
            pltpu.VMEM((NZ, 2, E, R), BF),
            pltpu.VMEM((NZ, E, R), BF),
            pltpu.VMEM((2, 4, E, R), BF),
            pltpu.VMEM((E, R), F32),
            pltpu.VMEM((E * E, R), BF),
            pltpu.VMEM((E * E, R), BF),
            pltpu.VMEM((TILES + 1, E, R), F32),
            pltpu.VMEM((TILES + 1, E, R), F32),
            pltpu.VMEM((16, E, R), BF),
            pltpu.VMEM((16, E, R), BF),
            pltpu.SMEM((1, R), jnp.int32),
            pltpu.SMEM((1, 1, 1, NZ), jnp.int32),
            pltpu.SMEM((1, 1, 1, TILES), jnp.int32),
            pltpu.SMEM((1, 1, 1, TILES), jnp.int32),
            pltpu.SMEM((1, 1, 1, TILES), jnp.int32),
            pltpu.SMEM((1, R), jnp.int32),
            pltpu.SMEM((1, 1, 1, TILES), jnp.int32),
            pltpu.SMEM((16,), jnp.int32),
            pltpu.SMEM((16,), jnp.int32),
            pltpu.SMEM((16,), jnp.int32),
            dma((TILES,)), dma((7,)), dma((64,)), dma((64,)),
            dma((TILES,)), dma((TILES,)), dma((16,)), dma((16,)),
        ],
        compiler_params=pltpu.CompilerParams(collective_id=0, has_side_effects=True, vmem_limit_bytes=32 << 20),
        name="mttkrp",
    )(*args)


def solution(mesh):
    return jax.shard_map(
        local,
        mesh=mesh,
        in_specs=(
            P("ia", "ja", "ka", None, None, None),
            P(("ia", "ja"), None, None),
            P(("ia", "ka"), None, None),
            P("ia", "ja", None),
            P("ia", "ja", "ka", None, None),
            P("ia", "ja", "ka", None),
            P("ia", "ja", "ka", None),
            P("ia", "ja", "ka", None),
            P("ia", "ja", "ka"),
        ),
        out_specs=P(("ia", "ja", "ka"), None, None),
        check_vma=False,
    )
```

```python
import jax
import jax.numpy as jnp
from jax import lax
from jax.experimental import pallas as pl
from jax.experimental.pallas import tpu as pltpu
from jax.sharding import PartitionSpec as P

MESH = pl.DeviceIdType.MESH
NZ, NX, NY, NC = 16, 4, 4, 2
TILES = 8
E = 64
R = 128
Q = E // NX
H = E // 2
BF = jnp.bfloat16
F32 = jnp.float32
NEAR = (0, 1, 15, 2, 14, 4, 12)
FAR = (3, 13, 5, 11, 6, 10, 7, 9, 8)
POS = {r: n for n, r in enumerate(NEAR + FAR)}
SPLIT = len(NEAR)


def kernel(
    tiles_hbm, item_hbm, word_hbm, send_hbm, slot_hbm, tword_hbm, user_hbm, heavy_s, count_s,
    out_ref,
    tiles, items, gath, table, words, light, relay, item32, krao_a, krao_b, contrib, pcontrib, plane_out, plane_in,
    send_s, slot_s, tword_s, user_s, pcount_s, puser_s, pos_s, inv_s, pinv_s,
    tile_sem, load_sem, ss, rs, t_send, t_recv, q_send, q_recv,
):
    i = lax.axis_index("ia")
    j = lax.axis_index("ja")
    k = lax.axis_index("ka")
    y = j // 2
    c = lax.rem(j, 2)
    chip = y * NX + k
    kq = pl.multiple_of(k * Q, Q)
    yq = pl.multiple_of(y * Q, Q)

    def zdev(d):
        return {"ia": lax.rem(i + (d % NZ), NZ)}

    def chip_dev(q):
        return {"ja": (q // NX) * 2 + c, "ka": lax.rem(q, NX)}

    other = {"ja": y * 2 + 1 - c}
    used = [0]

    def remote(src, dst, device):
        n = used[0]
        used[0] += 1
        return pltpu.make_async_remote_copy(
            src_ref=src, dst_ref=dst, send_sem=ss.at[n], recv_sem=rs.at[n], device_id=device, device_id_type=MESH
        )

    load_items = pltpu.make_async_copy(item_hbm, items, load_sem.at[0])
    load_word = pltpu.make_async_copy(word_hbm.at[c, pl.ds(yq, Q)], gath.at[0, 1], load_sem.at[1])
    ints = ((send_hbm, send_s), (slot_hbm, slot_s), (tword_hbm, tword_s), (user_hbm, user_s))
    ints = [pltpu.make_async_copy(a, b, load_sem.at[2 + n]) for n, (a, b) in enumerate(ints)]
    for cp in ints:
        cp.start()
    load_items.start()
    load_word.start()

    barrier = pltpu.get_barrier_semaphore()
    for d in (4, -4, 3, -3, 2, -2, 1, -1):
        pl.semaphore_signal(barrier, inc=1, device_id=zdev(d), device_id_type=MESH)
    for d in range(1, 16):
        pl.semaphore_signal(barrier, inc=1, device_id=chip_dev(lax.rem(chip + d, 16)), device_id_type=MESH)
    pl.semaphore_signal(barrier, inc=1, device_id=other, device_id_type=MESH)

    tile_loads = [pltpu.make_async_copy(tiles_hbm.at[0, 0, 0, t], tiles.at[t], tile_sem.at[t]) for t in range(TILES)]
    for cp in tile_loads:
        cp.start()
    for r, n in POS.items():
        pos_s[r] = n

    for cp in ints:
        cp.wait()
    load_items.wait()
    load_word.wait()
    gath[0, 0] = items[heavy_s[0, 0, 0], pl.ds(kq, Q), :]
    for d in range(1, NZ):
        light[d] = items[send_s[0, 0, 0, lax.rem(i + d, NZ)]]
    table[NZ] = items[send_s[0, 0, 0, i]]

    def find(live, user, inv):
        count = live[0, 0, 0]

        def body(n, carry):
            u = (n // NX) * (NC * NX) + c * NX + lax.rem(n, NX)
            at = jnp.int32(TILES)
            for t in range(TILES):
                at = jnp.where((user[0, 0, 0, t] == u) & (count > t), t, at)
            inv[n] = at
            return carry

        lax.fori_loop(0, NX * NY, body, 0)


    pl.semaphore_wait(barrier, 24)

    def direct(d):
        return remote(gath.at[0], gath.at[POS[-d % NZ]], zdev(d))

    ag = {-d % NZ: direct(d) for d in (4, -4, 2, -2, 1, -1)}
    for cp in ag.values():
        cp.start()

    up = [remote(light.at[8, pl.ds(0, H)], relay.at[0, 3, pl.ds(0, H)], zdev(4))]
    down = [remote(light.at[8, pl.ds(H, H)], relay.at[1, 3, pl.ds(H, H)], zdev(-4))]
    for f in (3, 2, 1):
        up.append(remote(light.at[4 + f], relay.at[0, f - 1], zdev(4)))
        down.append(remote(light.at[NZ - 4 - f], relay.at[1, f - 1], zdev(-4)))
    for a, b in zip(up, down):
        a.start()
        b.start()
    px = [remote(count_s, pcount_s, other), remote(user_hbm, puser_s, other)]
    for cp in px:
        cp.start()
    find(count_s, user_s, inv_s)
    contrib[TILES] = jnp.zeros((E, R), F32)
    pcontrib[TILES] = jnp.zeros((E, R), F32)

    ag[12].wait_recv()
    ag[4].wait_recv()
    hops = [
        remote(gath.at[POS[12], 0], gath.at[POS[8], 0], zdev(4)),
        remote(gath.at[POS[4], 1], gath.at[POS[8], 1], zdev(-4)),
    ]
    for f in (3, 2, 1):
        hops.append(remote(gath.at[POS[12]], gath.at[POS[12 - f]], zdev(f)))
        hops.append(remote(gath.at[POS[4]], gath.at[POS[4 + f]], zdev(-f)))
    hops.append(remote(gath.at[POS[12]], gath.at[POS[13]], zdev(-1)))
    hops.append(remote(gath.at[POS[4]], gath.at[POS[3]], zdev(1)))
    for cp in hops:
        cp.start()

    near = [remote(light.at[d % NZ], table.at[NZ + (-d % NZ)], zdev(d)) for d in (4, -4, 3, -3, 2, -2, 1, -1)]
    for cp in near:
        cp.start()

    def spread(lo, n):
        out = []
        for d in (2, 1, 3):
            out.append(
                remote(
                    gath.at[pl.ds(lo, n), 1], words.at[pl.ds(lo, n), c, pl.ds(yq, Q)], {"ja": lax.rem(j + 2 * d, NY * NC)}
                )
            )
            out.append(
                remote(gath.at[pl.ds(lo, n), 0], table.at[pl.ds(lo, n), pl.ds(kq, Q)], {"ka": lax.rem(k + d, NX)})
            )
        for cp in out:
            cp.start()
        for n in range(lo, lo + n):
            table[n, pl.ds(kq, Q), :] = gath[n, 0]
            words[n, c, pl.ds(yq, Q), :] = gath[n, 1]
        return out

    for r in (14, 2, 15, 1):
        ag[r].wait_recv()
    spread_a = spread(0, SPLIT)

    fwd = []
    for n, f in enumerate((4, 3, 2, 1)):
        rows = (pl.ds(0, H), pl.ds(H, H)) if f == 4 else (pl.ds(0, E), pl.ds(0, E))
        up[n].wait_recv()
        fwd.append(remote(relay.at[0, f - 1, rows[0]], table.at[NZ + 12 - f, rows[0]], zdev(f)))
        fwd[-1].start()
        down[n].wait_recv()
        fwd.append(remote(relay.at[1, f - 1, rows[1]], table.at[NZ + 4 + f, rows[1]], zdev(-f)))
        fwd[-1].start()

    for cp in hops:
        cp.wait_recv()
    spread_b = spread(SPLIT, NZ - SPLIT)

    def pair_words(sent, lo, n):
        for cp in sent[0::2]:
            cp.wait_recv()
        cp = remote(words.at[pl.ds(lo, n), c], words.at[pl.ds(lo, n), c], other)
        cp.start()
        return cp

    pw = [pair_words(spread_a, 0, SPLIT), pair_words(spread_b, SPLIT, NZ - SPLIT)]
    for cp in px:
        cp.wait_recv()
    find(pcount_s, puser_s, pinv_s)
    for cp in spread_a[1::2] + spread_b[1::2] + near + fwd + pw:
        cp.wait_recv()
    for cp in tile_loads:
        cp.wait()

    def build(t, krao):
        s = slot_s[0, 0, 0, t]
        r = (s - i) & (NZ - 1)
        item32[...] = table[jnp.where(s < NZ, pos_s[r], NZ + r)].astype(F32)
        q = tword_s[0, 0, 0, t]
        word = words[pos_s[((q >> 1) - i) & (NZ - 1)], q & 1]
        for b in range(E):
            row = jnp.broadcast_to(item32[pl.ds(b, 1), :], (E, R)).astype(BF)
            krao[pl.ds(b * E, E), :] = row * word

    groups = ((0, 4), (4, 8))

    def send_tiles(n):
        lo, hi = groups[n]
        return pltpu.make_async_remote_copy(
            src_ref=contrib.at[pl.ds(lo, hi - lo)], dst_ref=pcontrib.at[pl.ds(lo, hi - lo)],
            send_sem=t_send.at[n], recv_sem=t_recv.at[n], device_id=other, device_id_type=MESH,
        )

    build(0, krao_a)
    for n, (lo, hi) in enumerate(groups):
        for t in range(lo, hi):
            now, later = (krao_a, krao_b) if t % 2 == 0 else (krao_b, krao_a)
            contrib[t] = jnp.dot(tiles[t], now[...], preferred_element_type=F32)
            if t + 1 < TILES:
                build(t + 1, later)
        send_tiles(n).start()
    for n in range(len(groups)):
        send_tiles(n).wait_recv()

    def plane(dy, dx):
        q = lax.rem(y + dy, NY) * NX + lax.rem(k + dx, NX)
        n = dy * NX + dx
        return n, q, pltpu.make_async_remote_copy(
            src_ref=plane_out.at[n], dst_ref=plane_in.at[n], send_sem=q_send.at[n], recv_sem=q_recv.at[n],
            device_id=chip_dev(q), device_id_type=MESH,
        )

    far_first = (
        (2, 2), (2, 1), (2, 3), (1, 2), (3, 2), (1, 1), (3, 3), (1, 3), (3, 1), (2, 0), (0, 2), (1, 0), (3, 0), (0, 1), (0, 3),
    )
    for at in far_first:
        n, q, cp = plane(*at)
        plane_out[n] = (contrib[inv_s[q]] + pcontrib[pinv_s[q]]).astype(BF)
        cp.start()
    total = contrib[inv_s[chip]] + pcontrib[pinv_s[chip]]
    for at in far_first[::-1]:
        n, _, cp = plane(*at)
        cp.wait_recv()
        total = total + plane_in[n].astype(F32)
    out_ref[0] = total

    for cp in list(ag.values()) + up + down + px + hops + near + spread_a + spread_b + fwd + pw:
        cp.wait_send()
    for n in range(len(groups)):
        send_tiles(n).wait_send()
    for at in far_first:
        plane(*at)[2].wait_send()


def local(tiles, items, word_rows, heavy, send, slot, tword, user, count):
    dma = pltpu.SemaphoreType.DMA
    ints = (send.reshape(1, 1, 1, NZ), slot, tword, user)
    args = [pltpu.with_memory_space_constraint(a, pltpu.HBM) for a in (tiles, items, word_rows, *ints)]
    args += [heavy, count]
    return pl.pallas_call(
        kernel,
        out_shape=pltpu.VMEM((1, E, R), F32),
        in_specs=[pl.BlockSpec(memory_space=pltpu.HBM)] * 7 + [pl.BlockSpec(memory_space=pltpu.SMEM)] * 2,
        out_specs=pl.BlockSpec(memory_space=pltpu.VMEM),
        scratch_shapes=[
            pltpu.VMEM((TILES, E, E * E), BF),
            pltpu.VMEM((8, E, R), BF),
            pltpu.VMEM((NZ, 2, Q, R), BF),
            pltpu.VMEM((2 * NZ, E, R), BF),
            pltpu.VMEM((NZ, 2, E, R), BF),
            pltpu.VMEM((NZ, E, R), BF),
            pltpu.VMEM((2, 4, E, R), BF),
            pltpu.VMEM((E, R), F32),
            pltpu.VMEM((E * E, R), BF),
            pltpu.VMEM((E * E, R), BF),
            pltpu.VMEM((TILES + 1, E, R), F32),
            pltpu.VMEM((TILES + 1, E, R), F32),
            pltpu.VMEM((16, E, R), BF),
            pltpu.VMEM((16, E, R), BF),
            pltpu.SMEM((1, 1, 1, NZ), jnp.int32),
            pltpu.SMEM((1, 1, 1, TILES), jnp.int32),
            pltpu.SMEM((1, 1, 1, TILES), jnp.int32),
            pltpu.SMEM((1, 1, 1, TILES), jnp.int32),
            pltpu.SMEM((1, 1, 1), jnp.int32),
            pltpu.SMEM((1, 1, 1, TILES), jnp.int32),
            pltpu.SMEM((16,), jnp.int32),
            pltpu.SMEM((16,), jnp.int32),
            pltpu.SMEM((16,), jnp.int32),
            dma((TILES,)), dma((6,)), dma((64,)), dma((64,)),
            dma((TILES,)), dma((TILES,)), dma((16,)), dma((16,)),
        ],
        compiler_params=pltpu.CompilerParams(collective_id=0, has_side_effects=True, vmem_limit_bytes=32 << 20),
        name="mttkrp",
    )(*args)


def solution(mesh):
    return jax.shard_map(
        local,
        mesh=mesh,
        in_specs=(
            P("ia", "ja", "ka", None, None, None),
            P(("ia", "ja"), None, None),
            P(("ia", "ka"), None, None),
            P("ia", "ja", None),
            P("ia", "ja", "ka", None, None),
            P("ia", "ja", "ka", None),
            P("ia", "ja", "ka", None),
            P("ia", "ja", "ka", None),
            P("ia", "ja", "ka"),
        ),
        out_specs=P(("ia", "ja", "ka"), None, None),
        check_vma=False,
    )
```

```python
import jax
import jax.numpy as jnp
from jax import lax
from jax.experimental import pallas as pl
from jax.experimental.pallas import tpu as pltpu
from jax.sharding import PartitionSpec as P

MESH = pl.DeviceIdType.MESH
NZ, NX, NY, NC = 16, 4, 4, 2
TILES = 8
E = 64
R = 128
Q = E // NX
H = E // 2
BF = jnp.bfloat16
F32 = jnp.float32
NEAR = (0, 1, 15, 2, 14, 4, 12)
FAR = (3, 13, 5, 11, 6, 10, 7, 9, 8)
POS = {r: n for n, r in enumerate(NEAR + FAR)}
SPLIT = len(NEAR)
PLANE = (
    (2, 2), (2, 1), (2, 3), (1, 2), (3, 2), (1, 1), (3, 3), (1, 3), (3, 1), (2, 0), (0, 2), (1, 0), (3, 0), (0, 1), (0, 3),
)


def kernel(
    tiles_hbm, item_hbm, word_hbm, send_hbm, slot_hbm, tword_hbm, user_hbm, heavy_s, count_s,
    out_ref,
    tiles, items, gath, table, words, light, relay, item32, krao_a, krao_b, contrib, pcontrib, plane_out, plane_in,
    send_s, slot_s, tword_s, user_s, pcount_s, puser_s, pos_s, inv_s, pinv_s,
    tile_sem, load_sem, ss, rs, t_send, t_recv, q_send, q_recv,
):
    i = lax.axis_index("ia")
    j = lax.axis_index("ja")
    k = lax.axis_index("ka")
    y = j // 2
    c = lax.rem(j, 2)
    chip = y * NX + k
    kq = pl.multiple_of(k * Q, Q)
    yq = pl.multiple_of(y * Q, Q)

    def zdev(d):
        return {"ia": lax.rem(i + (d % NZ), NZ)}

    def chip_dev(q):
        return {"ja": (q // NX) * 2 + c, "ka": lax.rem(q, NX)}

    other = {"ja": y * 2 + 1 - c}
    used = [0]

    def remote(src, dst, device):
        n = used[0]
        used[0] += 1
        return pltpu.make_async_remote_copy(
            src_ref=src, dst_ref=dst, send_sem=ss.at[n], recv_sem=rs.at[n], device_id=device, device_id_type=MESH
        )

    load_items = pltpu.make_async_copy(item_hbm, items, load_sem.at[0])
    load_word = pltpu.make_async_copy(word_hbm.at[c, pl.ds(yq, Q)], gath.at[0, 1], load_sem.at[1])
    barrier = pltpu.get_barrier_semaphore()

    def greet(device):
        pl.semaphore_signal(barrier, inc=1, device_id=device, device_id_type=MESH)

    greet(zdev(4))
    greet(zdev(-4))
    for n, (dy, dx) in enumerate(PLANE):
        greet(chip_dev(lax.rem(y + dy, NY) * NX + lax.rem(k + dx, NX)))
        if n in (0, 4, 8):
            greet(zdev(3 - n // 4))
            greet(zdev(n // 4 - 3))
    greet(other)

    ints = ((send_hbm, send_s), (slot_hbm, slot_s), (tword_hbm, tword_s), (user_hbm, user_s))
    ints = [pltpu.make_async_copy(a, b, load_sem.at[2 + n]) for n, (a, b) in enumerate(ints)]
    for cp in ints:
        cp.start()
    load_items.start()
    load_word.start()

    tile_loads = [pltpu.make_async_copy(tiles_hbm.at[0, 0, 0, t], tiles.at[t], tile_sem.at[t]) for t in range(TILES)]
    for cp in tile_loads:
        cp.start()
    for r, n in POS.items():
        pos_s[r] = n

    for cp in ints:
        cp.wait()
    load_items.wait()
    load_word.wait()
    gath[0, 0] = items[heavy_s[0, 0, 0], pl.ds(kq, Q), :]
    for d in range(1, NZ):
        light[d] = items[send_s[0, 0, 0, lax.rem(i + d, NZ)]]
    table[NZ] = items[send_s[0, 0, 0, i]]

    def find(live, user, inv):
        count = live[0, 0, 0]

        def body(n, carry):
            u = (n // NX) * (NC * NX) + c * NX + lax.rem(n, NX)
            at = jnp.int32(TILES)
            for t in range(TILES):
                at = jnp.where((user[0, 0, 0, t] == u) & (count > t), t, at)
            inv[n] = at
            return carry

        lax.fori_loop(0, NX * NY, body, 0)


    pl.semaphore_wait(barrier, 24)

    def direct(d):
        return remote(gath.at[0], gath.at[POS[-d % NZ]], zdev(d))

    ag = {-d % NZ: direct(d) for d in (4, -4, 2, -2, 1, -1)}
    for cp in ag.values():
        cp.start()

    up = [remote(light.at[8, pl.ds(0, H)], relay.at[0, 3, pl.ds(0, H)], zdev(4))]
    down = [remote(light.at[8, pl.ds(H, H)], relay.at[1, 3, pl.ds(H, H)], zdev(-4))]
    for f in (3, 2, 1):
        up.append(remote(light.at[4 + f], relay.at[0, f - 1], zdev(4)))
        down.append(remote(light.at[NZ - 4 - f], relay.at[1, f - 1], zdev(-4)))
    for a, b in zip(up, down):
        a.start()
        b.start()
    px = [remote(count_s, pcount_s, other), remote(user_hbm, puser_s, other)]
    for cp in px:
        cp.start()
    find(count_s, user_s, inv_s)
    contrib[TILES] = jnp.zeros((E, R), F32)
    pcontrib[TILES] = jnp.zeros((E, R), F32)

    ag[12].wait_recv()
    ag[4].wait_recv()
    hops = [
        remote(gath.at[POS[12], 0], gath.at[POS[8], 0], zdev(4)),
        remote(gath.at[POS[4], 1], gath.at[POS[8], 1], zdev(-4)),
    ]
    for f in (3, 2, 1):
        hops.append(remote(gath.at[POS[12]], gath.at[POS[12 - f]], zdev(f)))
        hops.append(remote(gath.at[POS[4]], gath.at[POS[4 + f]], zdev(-f)))
    hops.append(remote(gath.at[POS[12]], gath.at[POS[13]], zdev(-1)))
    hops.append(remote(gath.at[POS[4]], gath.at[POS[3]], zdev(1)))
    for cp in hops:
        cp.start()

    near = [remote(light.at[d % NZ], table.at[NZ + (-d % NZ)], zdev(d)) for d in (4, -4, 3, -3, 2, -2, 1, -1)]
    for cp in near:
        cp.start()

    def spread(lo, n):
        out = []
        for d in (2, 1, 3):
            out.append(
                remote(
                    gath.at[pl.ds(lo, n), 1], words.at[pl.ds(lo, n), c, pl.ds(yq, Q)], {"ja": lax.rem(j + 2 * d, NY * NC)}
                )
            )
            out.append(
                remote(gath.at[pl.ds(lo, n), 0], table.at[pl.ds(lo, n), pl.ds(kq, Q)], {"ka": lax.rem(k + d, NX)})
            )
        for cp in out:
            cp.start()
        for n in range(lo, lo + n):
            table[n, pl.ds(kq, Q), :] = gath[n, 0]
            words[n, c, pl.ds(yq, Q), :] = gath[n, 1]
        return out

    for r in (14, 2, 15, 1):
        ag[r].wait_recv()
    spread_a = spread(0, SPLIT)

    fwd = []
    for n, f in enumerate((4, 3, 2, 1)):
        rows = (pl.ds(0, H), pl.ds(H, H)) if f == 4 else (pl.ds(0, E), pl.ds(0, E))
        up[n].wait_recv()
        fwd.append(remote(relay.at[0, f - 1, rows[0]], table.at[NZ + 12 - f, rows[0]], zdev(f)))
        fwd[-1].start()
        down[n].wait_recv()
        fwd.append(remote(relay.at[1, f - 1, rows[1]], table.at[NZ + 4 + f, rows[1]], zdev(-f)))
        fwd[-1].start()

    for cp in hops:
        cp.wait_recv()
    spread_b = spread(SPLIT, NZ - SPLIT)

    def pair_words(sent, lo, n):
        for cp in sent[0::2]:
            cp.wait_recv()
        cp = remote(words.at[pl.ds(lo, n), c], words.at[pl.ds(lo, n), c], other)
        cp.start()
        return cp

    pw = [pair_words(spread_a, 0, SPLIT), pair_words(spread_b, SPLIT, NZ - SPLIT)]
    for cp in px:
        cp.wait_recv()
    find(pcount_s, puser_s, pinv_s)
    for cp in spread_a[1::2] + spread_b[1::2] + near + fwd + pw:
        cp.wait_recv()
    for cp in tile_loads:
        cp.wait()

    def build(t, krao):
        s = slot_s[0, 0, 0, t]
        r = (s - i) & (NZ - 1)
        item32[...] = table[jnp.where(s < NZ, pos_s[r], NZ + r)].astype(F32)
        q = tword_s[0, 0, 0, t]
        word = words[pos_s[((q >> 1) - i) & (NZ - 1)], q & 1]
        for b in range(E):
            row = jnp.broadcast_to(item32[pl.ds(b, 1), :], (E, R)).astype(BF)
            krao[pl.ds(b * E, E), :] = row * word

    groups = ((0, 4), (4, 8))

    def send_tiles(n):
        lo, hi = groups[n]
        return pltpu.make_async_remote_copy(
            src_ref=contrib.at[pl.ds(lo, hi - lo)], dst_ref=pcontrib.at[pl.ds(lo, hi - lo)],
            send_sem=t_send.at[n], recv_sem=t_recv.at[n], device_id=other, device_id_type=MESH,
        )

    build(0, krao_a)
    for n, (lo, hi) in enumerate(groups):
        for t in range(lo, hi):
            now, later = (krao_a, krao_b) if t % 2 == 0 else (krao_b, krao_a)
            contrib[t] = jnp.dot(tiles[t], now[...], preferred_element_type=F32)
            if t + 1 < TILES:
                build(t + 1, later)
        send_tiles(n).start()
    for n in range(len(groups)):
        send_tiles(n).wait_recv()

    def plane(dy, dx):
        q = lax.rem(y + dy, NY) * NX + lax.rem(k + dx, NX)
        n = dy * NX + dx
        return n, q, pltpu.make_async_remote_copy(
            src_ref=plane_out.at[n], dst_ref=plane_in.at[n], send_sem=q_send.at[n], recv_sem=q_recv.at[n],
            device_id=chip_dev(q), device_id_type=MESH,
        )

    for at in PLANE:
        n, q, cp = plane(*at)
        plane_out[n] = (contrib[inv_s[q]] + pcontrib[pinv_s[q]]).astype(BF)
        cp.start()
    total = contrib[inv_s[chip]] + pcontrib[pinv_s[chip]]
    for at in PLANE[::-1]:
        n, _, cp = plane(*at)
        cp.wait_recv()
        total = total + plane_in[n].astype(F32)
    out_ref[0] = total

    for cp in list(ag.values()) + up + down + px + hops + near + spread_a + spread_b + fwd + pw:
        cp.wait_send()
    for n in range(len(groups)):
        send_tiles(n).wait_send()
    for at in PLANE:
        plane(*at)[2].wait_send()


def local(tiles, items, word_rows, heavy, send, slot, tword, user, count):
    dma = pltpu.SemaphoreType.DMA
    ints = (send.reshape(1, 1, 1, NZ), slot, tword, user)
    args = [pltpu.with_memory_space_constraint(a, pltpu.HBM) for a in (tiles, items, word_rows, *ints)]
    args += [heavy, count]
    return pl.pallas_call(
        kernel,
        out_shape=pltpu.VMEM((1, E, R), F32),
        in_specs=[pl.BlockSpec(memory_space=pltpu.HBM)] * 7 + [pl.BlockSpec(memory_space=pltpu.SMEM)] * 2,
        out_specs=pl.BlockSpec(memory_space=pltpu.VMEM),
        scratch_shapes=[
            pltpu.VMEM((TILES, E, E * E), BF),
            pltpu.VMEM((8, E, R), BF),
            pltpu.VMEM((NZ, 2, Q, R), BF),
            pltpu.VMEM((2 * NZ, E, R), BF),
            pltpu.VMEM((NZ, 2, E, R), BF),
            pltpu.VMEM((NZ, E, R), BF),
            pltpu.VMEM((2, 4, E, R), BF),
            pltpu.VMEM((E, R), F32),
            pltpu.VMEM((E * E, R), BF),
            pltpu.VMEM((E * E, R), BF),
            pltpu.VMEM((TILES + 1, E, R), F32),
            pltpu.VMEM((TILES + 1, E, R), F32),
            pltpu.VMEM((16, E, R), BF),
            pltpu.VMEM((16, E, R), BF),
            pltpu.SMEM((1, 1, 1, NZ), jnp.int32),
            pltpu.SMEM((1, 1, 1, TILES), jnp.int32),
            pltpu.SMEM((1, 1, 1, TILES), jnp.int32),
            pltpu.SMEM((1, 1, 1, TILES), jnp.int32),
            pltpu.SMEM((1, 1, 1), jnp.int32),
            pltpu.SMEM((1, 1, 1, TILES), jnp.int32),
            pltpu.SMEM((16,), jnp.int32),
            pltpu.SMEM((16,), jnp.int32),
            pltpu.SMEM((16,), jnp.int32),
            dma((TILES,)), dma((6,)), dma((64,)), dma((64,)),
            dma((TILES,)), dma((TILES,)), dma((16,)), dma((16,)),
        ],
        compiler_params=pltpu.CompilerParams(collective_id=0, has_side_effects=True, vmem_limit_bytes=32 << 20),
        name="mttkrp",
    )(*args)


def solution(mesh):
    return jax.shard_map(
        local,
        mesh=mesh,
        in_specs=(
            P("ia", "ja", "ka", None, None, None),
            P(("ia", "ja"), None, None),
            P(("ia", "ka"), None, None),
            P("ia", "ja", None),
            P("ia", "ja", "ka", None, None),
            P("ia", "ja", "ka", None),
            P("ia", "ja", "ka", None),
            P("ia", "ja", "ka", None),
            P("ia", "ja", "ka"),
        ),
        out_specs=P(("ia", "ja", "ka"), None, None),
        check_vma=False,
    )
```

```python
import jax
import jax.numpy as jnp
from jax import lax
from jax.experimental import pallas as pl
from jax.experimental.pallas import tpu as pltpu
from jax.sharding import PartitionSpec as P

MESH = pl.DeviceIdType.MESH
NZ, NX, NY, NC = 16, 4, 4, 2
TILES = 8
E = 64
R = 128
Q = E // NX
H = E // 2
BF = jnp.bfloat16
F32 = jnp.float32
NEAR = (0, 1, 15, 2, 14, 4, 12)
FAR = (3, 13, 5, 11, 6, 10, 7, 9, 8)
POS = {r: n for n, r in enumerate(NEAR + FAR)}
SPLIT = len(NEAR)
PLANE = (
    (2, 2), (2, 1), (2, 3), (1, 2), (3, 2), (1, 1), (3, 3), (1, 3), (3, 1), (2, 0), (0, 2), (1, 0), (3, 0), (0, 1), (0, 3),
)


def kernel(
    tiles_hbm, item_hbm, word_hbm, send_hbm, slot_hbm, tword_hbm, user_hbm, heavy_s, count_s,
    out_ref,
    tiles, items, gath, table, words, light, relay, item32, krao_a, krao_b, contrib, pcontrib, plane_out, plane_in,
    send_s, slot_s, tword_s, user_s, pcount_s, puser_s, pos_s, inv_s, pinv_s,
    tile_sem, load_sem, ss, rs, t_send, t_recv, q_send, q_recv,
):
    i = lax.axis_index("ia")
    j = lax.axis_index("ja")
    k = lax.axis_index("ka")
    y = j // 2
    c = lax.rem(j, 2)
    chip = y * NX + k
    kq = pl.multiple_of(k * Q, Q)
    yq = pl.multiple_of(y * Q, Q)

    def zdev(d):
        return {"ia": lax.rem(i + (d % NZ), NZ)}

    def chip_dev(q):
        return {"ja": (q // NX) * 2 + c, "ka": lax.rem(q, NX)}

    other = {"ja": y * 2 + 1 - c}
    used = [0]

    def remote(src, dst, device):
        n = used[0]
        used[0] += 1
        return pltpu.make_async_remote_copy(
            src_ref=src, dst_ref=dst, send_sem=ss.at[n], recv_sem=rs.at[n], device_id=device, device_id_type=MESH
        )

    load_items = pltpu.make_async_copy(item_hbm, items, load_sem.at[0])
    load_word = pltpu.make_async_copy(word_hbm.at[c, pl.ds(yq, Q)], gath.at[0, 1], load_sem.at[1])
    barrier = pltpu.get_barrier_semaphore()

    def greet(device):
        pl.semaphore_signal(barrier, inc=1, device_id=device, device_id_type=MESH)

    greet(zdev(4))
    greet(zdev(-4))
    for n, (dy, dx) in enumerate(PLANE):
        greet(chip_dev(lax.rem(y + dy, NY) * NX + lax.rem(k + dx, NX)))
        if n in (0, 4, 8):
            greet(zdev(3 - n // 4))
            greet(zdev(n // 4 - 3))
    greet(other)

    ints = ((send_hbm, send_s), (slot_hbm, slot_s), (tword_hbm, tword_s), (user_hbm, user_s))
    ints = [pltpu.make_async_copy(a, b, load_sem.at[2 + n]) for n, (a, b) in enumerate(ints)]
    for cp in ints:
        cp.start()
    load_items.start()
    load_word.start()

    tile_loads = [pltpu.make_async_copy(tiles_hbm.at[0, 0, 0, t], tiles.at[t], tile_sem.at[t]) for t in range(TILES)]
    for cp in tile_loads:
        cp.start()
    for r, n in POS.items():
        pos_s[r] = n

    for cp in ints:
        cp.wait()
    load_items.wait()
    load_word.wait()
    gath[0, 0] = items[heavy_s[0, 0, 0], pl.ds(kq, Q), :]
    for d in range(1, NZ):
        light[d] = items[send_s[0, 0, 0, lax.rem(i + d, NZ)]]
    table[NZ] = items[send_s[0, 0, 0, i]]

    def find(live, user, inv):
        count = live[0, 0, 0]

        def body(n, carry):
            u = (n // NX) * (NC * NX) + c * NX + lax.rem(n, NX)
            at = jnp.int32(TILES)
            for t in range(TILES):
                at = jnp.where((user[0, 0, 0, t] == u) & (count > t), t, at)
            inv[n] = at
            return carry

        lax.fori_loop(0, NX * NY, body, 0)


    pl.semaphore_wait(barrier, 24)

    def direct(d):
        return remote(gath.at[0], gath.at[POS[-d % NZ]], zdev(d))

    ag = {-d % NZ: direct(d) for d in (4, -4, 2, -2, 1, -1)}
    for cp in ag.values():
        cp.start()

    up = [remote(light.at[8, pl.ds(0, H)], relay.at[0, 3, pl.ds(0, H)], zdev(4))]
    down = [remote(light.at[8, pl.ds(H, H)], relay.at[1, 3, pl.ds(H, H)], zdev(-4))]
    for f in (3, 2, 1):
        up.append(remote(light.at[4 + f], relay.at[0, f - 1], zdev(4)))
        down.append(remote(light.at[NZ - 4 - f], relay.at[1, f - 1], zdev(-4)))
    for a, b in zip(up[:2], down[:2]):
        a.start()
        b.start()
    px = [remote(count_s, pcount_s, other), remote(user_hbm, puser_s, other)]
    for cp in px:
        cp.start()
    find(count_s, user_s, inv_s)
    contrib[TILES] = jnp.zeros((E, R), F32)
    pcontrib[TILES] = jnp.zeros((E, R), F32)

    ag[12].wait_recv()
    ag[4].wait_recv()
    hops = [
        remote(gath.at[POS[12], 0], gath.at[POS[8], 0], zdev(4)),
        remote(gath.at[POS[4], 1], gath.at[POS[8], 1], zdev(-4)),
    ]
    for f in (3, 2, 1):
        hops.append(remote(gath.at[POS[12]], gath.at[POS[12 - f]], zdev(f)))
        hops.append(remote(gath.at[POS[4]], gath.at[POS[4 + f]], zdev(-f)))
    hops.append(remote(gath.at[POS[12]], gath.at[POS[13]], zdev(-1)))
    hops.append(remote(gath.at[POS[4]], gath.at[POS[3]], zdev(1)))
    for cp in hops:
        cp.start()

    for a, b in zip(up[2:], down[2:]):
        a.start()
        b.start()
    near = [remote(light.at[d % NZ], table.at[NZ + (-d % NZ)], zdev(d)) for d in (4, -4, 3, -3, 2, -2, 1, -1)]
    for cp in near:
        cp.start()

    def spread(lo, n):
        out = []
        for d in (2, 1, 3):
            out.append(
                remote(
                    gath.at[pl.ds(lo, n), 1], words.at[pl.ds(lo, n), c, pl.ds(yq, Q)], {"ja": lax.rem(j + 2 * d, NY * NC)}
                )
            )
            out.append(
                remote(gath.at[pl.ds(lo, n), 0], table.at[pl.ds(lo, n), pl.ds(kq, Q)], {"ka": lax.rem(k + d, NX)})
            )
        for cp in out:
            cp.start()
        for n in range(lo, lo + n):
            table[n, pl.ds(kq, Q), :] = gath[n, 0]
            words[n, c, pl.ds(yq, Q), :] = gath[n, 1]
        return out

    for r in (14, 2, 15, 1):
        ag[r].wait_recv()
    spread_a = spread(0, SPLIT)

    fwd = []
    for n, f in enumerate((4, 3, 2, 1)):
        rows = (pl.ds(0, H), pl.ds(H, H)) if f == 4 else (pl.ds(0, E), pl.ds(0, E))
        up[n].wait_recv()
        fwd.append(remote(relay.at[0, f - 1, rows[0]], table.at[NZ + 12 - f, rows[0]], zdev(f)))
        fwd[-1].start()
        down[n].wait_recv()
        fwd.append(remote(relay.at[1, f - 1, rows[1]], table.at[NZ + 4 + f, rows[1]], zdev(-f)))
        fwd[-1].start()

    for cp in hops:
        cp.wait_recv()
    spread_b = spread(SPLIT, NZ - SPLIT)

    def pair_words(sent, lo, n):
        for cp in sent[0::2]:
            cp.wait_recv()
        cp = remote(words.at[pl.ds(lo, n), c], words.at[pl.ds(lo, n), c], other)
        cp.start()
        return cp

    pw = [pair_words(spread_a, 0, SPLIT), pair_words(spread_b, SPLIT, NZ - SPLIT)]
    for cp in px:
        cp.wait_recv()
    find(pcount_s, puser_s, pinv_s)
    for cp in spread_a[1::2] + spread_b[1::2] + near + fwd + pw:
        cp.wait_recv()
    for cp in tile_loads:
        cp.wait()

    def build(t, krao):
        s = slot_s[0, 0, 0, t]
        r = (s - i) & (NZ - 1)
        item32[...] = table[jnp.where(s < NZ, pos_s[r], NZ + r)].astype(F32)
        q = tword_s[0, 0, 0, t]
        word = words[pos_s[((q >> 1) - i) & (NZ - 1)], q & 1]
        for b in range(E):
            row = jnp.broadcast_to(item32[pl.ds(b, 1), :], (E, R)).astype(BF)
            krao[pl.ds(b * E, E), :] = row * word

    groups = ((0, 4), (4, 8))

    def send_tiles(n):
        lo, hi = groups[n]
        return pltpu.make_async_remote_copy(
            src_ref=contrib.at[pl.ds(lo, hi - lo)], dst_ref=pcontrib.at[pl.ds(lo, hi - lo)],
            send_sem=t_send.at[n], recv_sem=t_recv.at[n], device_id=other, device_id_type=MESH,
        )

    build(0, krao_a)
    for n, (lo, hi) in enumerate(groups):
        for t in range(lo, hi):
            now, later = (krao_a, krao_b) if t % 2 == 0 else (krao_b, krao_a)
            contrib[t] = jnp.dot(tiles[t], now[...], preferred_element_type=F32)
            if t + 1 < TILES:
                build(t + 1, later)
        send_tiles(n).start()
    for n in range(len(groups)):
        send_tiles(n).wait_recv()

    def plane(dy, dx):
        q = lax.rem(y + dy, NY) * NX + lax.rem(k + dx, NX)
        n = dy * NX + dx
        return n, q, pltpu.make_async_remote_copy(
            src_ref=plane_out.at[n], dst_ref=plane_in.at[n], send_sem=q_send.at[n], recv_sem=q_recv.at[n],
            device_id=chip_dev(q), device_id_type=MESH,
        )

    for at in PLANE:
        n, q, cp = plane(*at)
        plane_out[n] = (contrib[inv_s[q]] + pcontrib[pinv_s[q]]).astype(BF)
        cp.start()
    total = contrib[inv_s[chip]] + pcontrib[pinv_s[chip]]
    for at in PLANE[::-1]:
        n, _, cp = plane(*at)
        cp.wait_recv()
        total = total + plane_in[n].astype(F32)
    out_ref[0] = total

    for cp in list(ag.values()) + up + down + px + hops + near + spread_a + spread_b + fwd + pw:
        cp.wait_send()
    for n in range(len(groups)):
        send_tiles(n).wait_send()
    for at in PLANE:
        plane(*at)[2].wait_send()


def local(tiles, items, word_rows, heavy, send, slot, tword, user, count):
    dma = pltpu.SemaphoreType.DMA
    ints = (send.reshape(1, 1, 1, NZ), slot, tword, user)
    args = [pltpu.with_memory_space_constraint(a, pltpu.HBM) for a in (tiles, items, word_rows, *ints)]
    args += [heavy, count]
    return pl.pallas_call(
        kernel,
        out_shape=pltpu.VMEM((1, E, R), F32),
        in_specs=[pl.BlockSpec(memory_space=pltpu.HBM)] * 7 + [pl.BlockSpec(memory_space=pltpu.SMEM)] * 2,
        out_specs=pl.BlockSpec(memory_space=pltpu.VMEM),
        scratch_shapes=[
            pltpu.VMEM((TILES, E, E * E), BF),
            pltpu.VMEM((8, E, R), BF),
            pltpu.VMEM((NZ, 2, Q, R), BF),
            pltpu.VMEM((2 * NZ, E, R), BF),
            pltpu.VMEM((NZ, 2, E, R), BF),
            pltpu.VMEM((NZ, E, R), BF),
            pltpu.VMEM((2, 4, E, R), BF),
            pltpu.VMEM((E, R), F32),
            pltpu.VMEM((E * E, R), BF),
            pltpu.VMEM((E * E, R), BF),
            pltpu.VMEM((TILES + 1, E, R), F32),
            pltpu.VMEM((TILES + 1, E, R), F32),
            pltpu.VMEM((16, E, R), BF),
            pltpu.VMEM((16, E, R), BF),
            pltpu.SMEM((1, 1, 1, NZ), jnp.int32),
            pltpu.SMEM((1, 1, 1, TILES), jnp.int32),
            pltpu.SMEM((1, 1, 1, TILES), jnp.int32),
            pltpu.SMEM((1, 1, 1, TILES), jnp.int32),
            pltpu.SMEM((1, 1, 1), jnp.int32),
            pltpu.SMEM((1, 1, 1, TILES), jnp.int32),
            pltpu.SMEM((16,), jnp.int32),
            pltpu.SMEM((16,), jnp.int32),
            pltpu.SMEM((16,), jnp.int32),
            dma((TILES,)), dma((6,)), dma((64,)), dma((64,)),
            dma((TILES,)), dma((TILES,)), dma((16,)), dma((16,)),
        ],
        compiler_params=pltpu.CompilerParams(collective_id=0, has_side_effects=True, vmem_limit_bytes=32 << 20),
        name="mttkrp",
    )(*args)


def solution(mesh):
    return jax.shard_map(
        local,
        mesh=mesh,
        in_specs=(
            P("ia", "ja", "ka", None, None, None),
            P(("ia", "ja"), None, None),
            P(("ia", "ka"), None, None),
            P("ia", "ja", None),
            P("ia", "ja", "ka", None, None),
            P("ia", "ja", "ka", None),
            P("ia", "ja", "ka", None),
            P("ia", "ja", "ka", None),
            P("ia", "ja", "ka"),
        ),
        out_specs=P(("ia", "ja", "ka"), None, None),
        check_vma=False,
    )
```
